32 devices in a mesh: replica: 16 (over z, y, x), tensor: 2 (over core).
Axes of the slice: x: 2, y: 2, z: 4, core: 2. Of those that a mesh axis runs over, the one named last changes fastest.
Arguments:
- queries: bfloat16 [2048, 4096], P('replica', 'tensor'), may hold values from -9 to 9
- new_kv: bfloat16 [2, 2048, 1024], P(None, 'replica', 'tensor'), may hold values from -16 to 16
- cache: bfloat16 [128, 2, 64, 1024], P('replica', None, None, 'tensor'), may hold values from -16 to 16
- block_owner: int32 [16, 64], replicated, may hold values from 0 to 15, as said below
- block_slot: int32 [16, 64], replicated, may hold values from 0 to 7, as said below
- prefix_blocks: int32 [16], replicated, may hold values from 1 to 64, 512 in all
- out_weight: bfloat16 [4096, 4096], P('tensor'), may hold values from -0.09375 to 0.09375
Outputs:
- mixed: bfloat16 [2048, 4096], P(('replica', 'tensor'))
The draws below stay inside these ranges and needn't reach their ends.
Inputs may be any that keep to these rules, and one draw needn't show every extreme that they name: `block_owner`: within one replica's row, every owner that appears does so exactly 4 times. `block_slot`: the 4 entries of one replica's row that name one owner name different slots. `prefix_blocks`: the largest is 64 in every draw.
All inputs are finite; a program needn't handle non-finite values.
Results may differ from the reference program's by a relative error of at most 0.024.
Values may be sent and summed in bfloat16 or wider, within the bound.
A program may use at most 128 MiB of HBM per device.

```python
import math
import jax
import jax.numpy as jnp
import numpy as np
from jax import lax

HQ = 32
KVH = 8
HD = 128
DW = 4096
BLOCK = 64
MAXB = 64
SLOTS = 8
TOK = 128
CAP = 4
TOKENS = 2048
POOL = 128
N_REPLICA = 16
N_TENSOR = 2


def value_scales(key, shape):
    return jnp.exp(jax.random.uniform(key, shape, jnp.float32, math.log(0.3), math.log(3.0)))


def table_pair(key):
    groups = MAXB // CAP

    def one_row(row_key):
        owner_key, slot_key, order_key = jax.random.split(row_key, 3)
        owners = jax.random.permutation(owner_key, N_REPLICA)[:groups].astype(jnp.int32)
        ranking = jax.random.randint(slot_key, (groups, SLOTS), 0, 1 << 20) * SLOTS + jnp.arange(SLOTS, dtype=jnp.int32)[None, :]
        slot_ids = jnp.argsort(ranking, axis=1, stable=True)[:, :CAP].astype(jnp.int32)
        order = jax.random.permutation(order_key, MAXB)
        return (jnp.repeat(owners, CAP)[order], slot_ids.reshape(-1)[order])
    return jax.vmap(one_row)(jax.random.split(key, N_REPLICA))


def draw_queries(key, part):
    key = jax.random.fold_in(key, 11)
    shape = (N_REPLICA, TOK // 32, 32, HQ, HD)
    base = jnp.clip(3.0 * jax.random.normal(key, shape, jnp.float32), -9.0, 9.0)
    return base.reshape(TOKENS, HQ * HD).astype(jnp.bfloat16)


def draw_new_kv(key, part):
    key = jax.random.fold_in(key, 12)
    key_part, value_part, scale_part = jax.random.split(key, 3)
    shape = (N_REPLICA, TOK // 32, 32, KVH, HD)
    scales = value_scales(scale_part, (N_REPLICA, TOK // 32, 32, KVH, 1))
    key_rows = jnp.clip(jax.random.normal(key_part, shape, jnp.float32), -5.0, 5.0)
    value_rows = jnp.clip(jax.random.normal(value_part, shape, jnp.float32), -5.0, 5.0) * scales
    return jnp.stack([key_rows, value_rows]).reshape(2, TOKENS, KVH * HD).astype(jnp.bfloat16)


def draw_cache(key, part):
    key = jax.random.fold_in(key, 13)
    key_part, value_part, scale_part = jax.random.split(key, 3)
    shape = (POOL, BLOCK, KVH, HD)
    scales = value_scales(scale_part, (POOL, BLOCK, KVH, 1))
    key_rows = jnp.clip(jax.random.normal(key_part, shape, jnp.float32), -5.0, 5.0)
    value_rows = jnp.clip(jax.random.normal(value_part, shape, jnp.float32), -5.0, 5.0) * scales
    return jnp.stack([key_rows, value_rows], axis=1).reshape(POOL, 2, BLOCK, KVH * HD).astype(jnp.bfloat16)


def draw_block_owner(key, part):
    owners, slot_ids = table_pair(key)
    return owners.astype(jnp.int32)


def draw_block_slot(key, part):
    owners, slot_ids = table_pair(key)
    return slot_ids.astype(jnp.int32)


def levels(key, dims, cuts, low, high):
    level, own = 1.0, jax.random.fold_in(key, 6)
    for position, blocks in cuts:
        draws = jnp.exp(jax.random.uniform(jax.random.fold_in(own, position), (blocks,), jnp.float32, low / len(cuts), high / len(cuts)))
        level = level * jnp.repeat(draws, dims[position] // blocks).reshape([-1 if axis == position else 1 for axis in range(len(dims))])
    return level


def length_profile(count, total, most, slope):
    portions = [(1 << 20) // math.isqrt(rank ** slope) + 1 for rank in range(2, count + 1)]
    spare, counts = total - most - (count - 1), [1] * (count - 1)
    while spare > 0:
        candidates = [i for i in range(count - 1) if counts[i] < most]
        mass, left = sum([portions[i] for i in candidates]), spare
        for i in candidates:
            addition = min(most - counts[i], max(1, left * portions[i] // mass), spare)
            counts[i] = counts[i] + addition
            spare = spare - addition
    return np.array([most] + counts)


def uneven(rng, count, total, reach, slope):
    if count == 2:
        one = jax.random.randint(rng, (), max(1, total - reach), min(reach, total - 1) + 1)
        return jnp.stack([one, total - one])
    sizes = jnp.asarray(length_profile(count, total, reach, slope), jnp.int32)
    twos = (count - 1) // 2
    donor, taker = sizes[1:1 + 2 * twos:2], sizes[2:2 + 2 * twos:2]
    slack = jnp.minimum(donor - 1, reach - taker)
    passed = jax.random.randint(jax.random.fold_in(rng, 1), (twos,), 0, 1 << 20) % (slack + 1)
    sizes = sizes.at[1:1 + 2 * twos:2].set(donor - passed).at[2:2 + 2 * twos:2].set(taker + passed)
    return sizes[jax.random.permutation(jax.random.fold_in(rng, 2), count)]


def centred(rng, dims, deviation, limit, shards=(), kind=jnp.bfloat16):
    values = jax.random.normal(rng, dims, jnp.float32) * deviation
    if len(shards) > 0:
        values = levels(rng, dims, shards, -0.22, 0.18) * values
    return jnp.clip(values, min=-limit, max=limit).astype(kind)


def setup_inputs(seed: int = 0) -> dict:
    seeds = jax.random.split(jax.random.key(seed), 8)
    queries = draw_queries(jax.random.fold_in(seeds[7], 71), 0)
    new_kv = draw_new_kv(jax.random.fold_in(seeds[7], 71), 0)
    cache = draw_cache(jax.random.fold_in(seeds[7], 71), 0)
    block_owner = draw_block_owner(jax.random.fold_in(seeds[7], 71), 0)
    block_slot = draw_block_slot(jax.random.fold_in(seeds[7], 71), 0)
    prefix_blocks = uneven(seeds[5], N_REPLICA, N_REPLICA * MAXB // 2, MAXB, 2).astype(jnp.int32)
    out_weight = centred(seeds[6], (HQ * HD, DW), (HQ * HD) ** -0.5, 0.09375, ((0, 2),))
    return {"queries": queries, "new_kv": new_kv, "cache": cache, "block_owner": block_owner, "block_slot": block_slot, "prefix_blocks": prefix_blocks, "out_weight": out_weight}


def reference(queries, new_kv, cache, block_owner, block_slot, prefix_blocks, out_weight):
    per_group = HQ // KVH
    scaling = HD ** -0.5
    prefix_len = MAXB * BLOCK
    weight_full = out_weight.astype(jnp.float32).reshape(N_TENSOR, HQ * HD // N_TENSOR, DW)

    def one_replica(replica):
        first_row = replica * TOK
        query_rows = lax.dynamic_slice_in_dim(queries, first_row, TOK, 0).astype(jnp.float32)
        query_rows = query_rows.reshape(TOK, KVH, per_group, HD)
        fresh = lax.dynamic_slice_in_dim(new_kv, first_row, TOK, 1)
        owners = lax.dynamic_index_in_dim(block_owner, replica, 0, keepdims=False)
        slot_ids = lax.dynamic_index_in_dim(block_slot, replica, 0, keepdims=False)
        blocks = cache[(owners * SLOTS + slot_ids).astype(jnp.int32)]
        key_rows = jnp.concatenate([blocks[:, 0].reshape(prefix_len, KVH * HD), fresh[0]], axis=0)
        key_rows = key_rows.astype(jnp.float32).reshape(prefix_len + TOK, KVH, HD)
        value_rows = jnp.concatenate([blocks[:, 1].reshape(prefix_len, KVH * HD), fresh[1]], axis=0)
        value_rows = value_rows.astype(jnp.float32).reshape(prefix_len + TOK, KVH, HD)
        scores = jnp.einsum("tkgd,skd->kgts", query_rows, key_rows) * scaling
        places = jnp.arange(prefix_len + TOK, dtype=jnp.int32)
        row_ids = jnp.arange(TOK, dtype=jnp.int32)
        length = lax.dynamic_index_in_dim(prefix_blocks, replica, 0, keepdims=False)
        allowed = jnp.where(places[None, :] < prefix_len,
                            places[None, :] < length * BLOCK,
                            places[None, :] - prefix_len <= row_ids[:, None])
        scores = jnp.where(allowed[None, None], scores, -jnp.inf)
        highest = jnp.max(scores, axis=3, keepdims=True)
        weights = jnp.exp(scores - highest)
        totals = jnp.sum(weights, axis=3)
        rounded = lax.optimization_barrier(weights.astype(jnp.bfloat16)).astype(jnp.float32)
        attended = jnp.einsum("kgts,skd->tkgd", rounded, value_rows) / jnp.transpose(totals, (2, 0, 1))[..., None]
        attended = attended.reshape(TOK, N_TENSOR, HQ * HD // N_TENSOR).astype(jnp.bfloat16)
        partials = jnp.einsum("tgc,gcn->gtn", attended.astype(jnp.float32), weight_full)
        partials = lax.optimization_barrier(partials.astype(jnp.bfloat16)).astype(jnp.float32)
        return jnp.sum(partials, axis=0).astype(jnp.bfloat16)

    mixed = lax.map(one_replica, jnp.arange(N_REPLICA, dtype=jnp.int32))
    return mixed.reshape(N_REPLICA * TOK, DW)
```

```python
import functools
import math

import jax
import jax.numpy as jnp
from jax import lax
from jax.experimental import pallas as pl
from jax.experimental.pallas import tpu as pltpu
from jax.sharding import PartitionSpec as P

HQ = 32
KVH = 8
HD = 128
BLOCK = 64
MAXB = 64
PER_GROUP = HQ // KVH

FLOOR = -1e29
MASKED = -2e30
MESH = pl.DeviceIdType.MESH


def block_tables(block_owner, block_slot, prefix_blocks, own, planes, members, capacity):
    plane, member = own // members, own % members
    rows = ((plane + jnp.arange(planes, dtype=jnp.int32)) % planes) * members + member
    owners = plane * members + (member + jnp.arange(members, dtype=jnp.int32)) % members
    places = jnp.arange(block_owner.shape[1], dtype=jnp.int32)
    owner_rows, slot_rows, lengths = block_owner[rows], block_slot[rows], prefix_blocks[rows]
    used = places[None, :] < lengths[:, None]
    chosen = (owner_rows[:, None, :] == owners[None, :, None]) & used[:, None, :]
    ranks = jnp.cumsum(chosen.astype(jnp.int32), axis=2) - 1
    levels = jnp.arange(capacity, dtype=jnp.int32)
    matches = chosen[:, :, None, :] & (ranks[:, :, None, :] == levels[None, None, :, None])
    slots = jnp.sum(jnp.where(matches, slot_rows[:, None, None, :], 0), axis=3)
    return slots.reshape(-1), jnp.sum(chosen.astype(jnp.int32), axis=2).reshape(-1)


def attend_kernel(
    planes, members, capacity, slots_ref, counts_ref, q_ref, new_ref, cache_ref, out_ref,
    qbuf, kvbuf, acc, stat, part_out, part_in, stat_in,
    q_send, q_recv, kv_send, kv_recv, p_send, p_recv, s_send, s_recv,
):
    own = lax.axis_index("replica")
    plane, member = lax.div(own, members), lax.rem(own, members)
    heads_kv, lanes = acc.shape[1], acc.shape[3]
    tokens = lanes // PER_GROUP
    factor = HD ** (-0.5) * math.log2(math.e)

    def column(i):
        return {"replica": lax.rem(plane + i, planes) * members + member}

    def in_plane(j):
        return {"replica": plane * members + lax.rem(member + j, members)}

    def q_copy(i):
        return pltpu.make_async_remote_copy(
            qbuf.at[0], qbuf.at[planes - i], q_send.at[i], q_recv.at[planes - i],
            device_id=column(i), device_id_type=MESH)

    def kv_copy(j):
        return pltpu.make_async_remote_copy(
            cache_ref, kvbuf[members - j - 1], kv_send.at[j], kv_recv.at[members - j],
            device_id=in_plane(j), device_id_type=MESH)

    def part_copy(i):
        return pltpu.make_async_remote_copy(
            part_out.at[i], part_in.at[planes - i], p_send.at[i], p_recv.at[planes - i],
            device_id=column(i), device_id_type=MESH)

    def stat_copy(i):
        return pltpu.make_async_remote_copy(
            stat.at[i], stat_in.at[planes - i], s_send.at[i], s_recv.at[planes - i],
            device_id=column(i), device_id_type=MESH)

    barrier = pltpu.get_barrier_semaphore()
    for i in range(1, planes):
        pl.semaphore_signal(barrier, inc=1, device_id=column(i), device_id_type=MESH)
    for j in range(1, members):
        pl.semaphore_signal(barrier, inc=1, device_id=in_plane(j), device_id_type=MESH)
    for head in range(heads_kv * PER_GROUP):
        k, g = divmod(head, PER_GROUP)
        qbuf[0, k, g * tokens:(g + 1) * tokens, :] = q_ref[:, head * HD:(head + 1) * HD]
    pl.semaphore_wait(barrier, planes + members - 2)

    for i in range(1, planes):
        q_copy(i).start()
    for j in range(1, members):
        kv_copy(j).start()

    def update(i, k, keys, values, allowed):
        scores = lax.dot_general(
            keys, qbuf[i, k], (((1,), (1,)), ((), ())), preferred_element_type=jnp.float32)
        scores = jnp.where(allowed, scores * factor, MASKED)
        before = stat[i, k:k + 1, :]
        highest = jnp.maximum(before, jnp.max(scores, axis=0, keepdims=True))
        weights = jnp.exp2(scores - highest)
        scale = jnp.exp2(before - highest)
        total = stat[i, heads_kv + k:heads_kv + k + 1, :]
        stat[i, heads_kv + k:heads_kv + k + 1, :] = (
            total * scale + jnp.sum(weights, axis=0, keepdims=True))
        stat[i, k:k + 1, :] = highest
        acc[i, k] = acc[i, k] * scale + lax.dot_general(
            values, weights.astype(jnp.bfloat16), (((0,), (0,)), ((), ())),
            preferred_element_type=jnp.float32)

    def fold(i, j):
        source = cache_ref if j == 0 else kvbuf[j - 1]
        pair = i * members + j
        slots = [slots_ref[pair * capacity + c] for c in range(capacity)]
        rows = lax.broadcasted_iota(jnp.int32, (capacity * BLOCK, lanes), 0)
        allowed = rows < counts_ref[pair] * BLOCK
        for k in range(heads_kv):
            cut = slice(k * HD, (k + 1) * HD)
            keys = jnp.concatenate([source[s, 0, :, cut] for s in slots], axis=0)
            values = jnp.concatenate([source[s, 1, :, cut] for s in slots], axis=0)
            update(i, k, keys, values, allowed)

    def clear(i, carry):
        acc[i] = jnp.zeros(acc.shape[1:], jnp.float32)
        stat[i, :heads_kv, :] = jnp.full((heads_kv, lanes), FLOOR, jnp.float32)
        stat[i, heads_kv:, :] = jnp.zeros((heads_kv, lanes), jnp.float32)
        return carry

    lax.fori_loop(0, planes, clear, 0)

    rows = lax.broadcasted_iota(jnp.int32, (tokens, lanes), 0)
    cols = lax.broadcasted_iota(jnp.int32, (tokens, lanes), 1)
    causal = rows <= cols % tokens
    for k in range(heads_kv):
        cut = slice(k * HD, (k + 1) * HD)
        update(0, k, new_ref[0, :, cut], new_ref[1, :, cut], causal)

    def arrived(i, carry):
        @pl.when(i > 0)
        def _():
            q_copy(planes - i).wait_recv()
        fold(i, 0)
        return carry

    lax.fori_loop(0, planes, arrived, 0)
    for j in range(1, members):
        kv_copy(members - j).wait_recv()

        def each(step, carry, j=j):
            i = planes - 1 - step
            fold(i, j)
            if j == members - 1:
                @pl.when(i > 0)
                def _():
                    part_out[i] = acc[i].astype(jnp.bfloat16)
                    part_copy(i).start()
                    stat_copy(i).start()
            return carry

        lax.fori_loop(0, planes, each, 0)

    for i in range(1, planes):
        part_copy(planes - i).wait_recv()
        stat_copy(planes - i).wait_recv()
    for k in range(heads_kv):
        maxima = [stat[0, k:k + 1, :]] + [stat_in[i, k:k + 1, :] for i in range(1, planes)]
        highest = functools.reduce(jnp.maximum, maxima)
        scales = [jnp.exp2(m - highest) for m in maxima]
        total = stat[0, heads_kv + k:heads_kv + k + 1, :] * scales[0]
        mixed = acc[0, k] * scales[0]
        for i in range(1, planes):
            total += stat_in[i, heads_kv + k:heads_kv + k + 1, :] * scales[i]
            mixed += part_in[i, k].astype(jnp.float32) * scales[i]
        mixed = mixed / total
        for g in range(PER_GROUP):
            head = k * PER_GROUP + g
            tile = mixed[:, g * tokens:(g + 1) * tokens]
            out_ref[:, head * HD:(head + 1) * HD] = tile.T.astype(jnp.bfloat16)

    for i in range(1, planes):
        q_copy(i).wait_send()
        part_copy(i).wait_send()
        stat_copy(i).wait_send()
    for j in range(1, members):
        kv_copy(j).wait_send()


def local(queries, new_kv, cache, block_owner, block_slot, prefix_blocks, out_weight):
    replicas = lax.axis_size("replica")
    own = lax.axis_index("replica")
    capacity = max(2, MAXB // replicas)
    planes = math.isqrt(replicas)
    members = replicas // planes
    tokens, heads_kv = queries.shape[0], cache.shape[3] // HD
    lanes = PER_GROUP * tokens
    slots, counts = block_tables(
        block_owner, block_slot, prefix_blocks, own, planes, members, capacity)
    part = (planes, heads_kv, HD, lanes)
    stats = (planes, 2 * heads_kv, lanes)
    vmem = pl.BlockSpec(memory_space=pltpu.VMEM)
    smem = pl.BlockSpec(memory_space=pltpu.SMEM)
    pairs = replicas * capacity * BLOCK * heads_kv * lanes
    attended = pl.pallas_call(
        functools.partial(attend_kernel, planes, members, capacity),
        out_shape=jax.ShapeDtypeStruct(queries.shape, jnp.bfloat16),
        in_specs=[smem, smem, vmem, vmem, vmem],
        out_specs=vmem,
        scratch_shapes=[
            pltpu.VMEM((planes, heads_kv, lanes, HD), jnp.bfloat16),
            [pltpu.VMEM(cache.shape, jnp.bfloat16) for _ in range(members - 1)],
            pltpu.VMEM(part, jnp.float32),
            pltpu.VMEM(stats, jnp.float32),
            pltpu.VMEM(part, jnp.bfloat16),
            pltpu.VMEM(part, jnp.bfloat16),
            pltpu.VMEM(stats, jnp.float32),
            pltpu.SemaphoreType.DMA((planes,)),
            pltpu.SemaphoreType.DMA((planes,)),
            pltpu.SemaphoreType.DMA((members,)),
            pltpu.SemaphoreType.DMA((members,)),
            pltpu.SemaphoreType.DMA((planes,)),
            pltpu.SemaphoreType.DMA((planes,)),
            pltpu.SemaphoreType.DMA((planes,)),
            pltpu.SemaphoreType.DMA((planes,)),
        ],
        compiler_params=pltpu.CompilerParams(
            collective_id=0, has_side_effects=True, vmem_limit_bytes=40 * 1024 * 1024),
        cost_estimate=pl.CostEstimate(
            flops=4 * pairs * HD, bytes_accessed=4 * cache.size, transcendentals=pairs),
    )(slots, counts, queries, new_kv, cache)
    return lax.psum_scatter(
        jnp.dot(attended, out_weight, preferred_element_type=jnp.float32).astype(jnp.bfloat16),
        "tensor",
        scatter_dimension=0,
        tiled=True,
    )


def solution(mesh):
    placed = (
        P("replica", "tensor"),
        P(None, "replica", "tensor"),
        P("replica", None, None, "tensor"),
        P(),
        P(),
        P(),
        P("tensor", None),
    )
    return jax.shard_map(
        local, mesh=mesh, in_specs=placed, out_specs=P(("replica", "tensor"), None), check_vma=False
    )
```

```python
import functools
import math

import jax
import jax.numpy as jnp
from jax import lax
from jax.experimental import pallas as pl
from jax.experimental.pallas import tpu as pltpu
from jax.sharding import PartitionSpec as P

HQ = 32
KVH = 8
HD = 128
BLOCK = 64
MAXB = 64
PER_GROUP = HQ // KVH

FLOOR = -1e29
MASKED = -2e30
MESH = pl.DeviceIdType.MESH


def block_tables(block_owner, block_slot, prefix_blocks, own, planes, members, capacity):
    plane, member = own // members, own % members
    rows = jnp.arange(planes, dtype=jnp.int32) * members + member
    owners = plane * members + jnp.stack(
        [plane_peer(member, j, members) for j in range(members)])
    places = jnp.arange(block_owner.shape[1], dtype=jnp.int32)
    owner_rows, slot_rows, lengths = block_owner[rows], block_slot[rows], prefix_blocks[rows]
    used = places[None, :] < lengths[:, None]
    chosen = (owner_rows[:, None, :] == owners[None, :, None]) & used[:, None, :]
    ranks = jnp.cumsum(chosen.astype(jnp.int32), axis=2) - 1
    levels = jnp.arange(capacity, dtype=jnp.int32)
    matches = chosen[:, :, None, :] & (ranks[:, :, None, :] == levels[None, None, :, None])
    slots = jnp.sum(jnp.where(matches, slot_rows[:, None, None, :], 0), axis=3)
    return slots.reshape(-1), jnp.sum(chosen.astype(jnp.int32), axis=2).reshape(-1)


def plane_peer(member, j, members):
    if members == 4:
        x, y = member % 2, member // 2
        return member + (j % 2) * (1 - 2 * x) + (j // 2) * (2 - 4 * y)
    return (member + j) % members


def attend_kernel(
    planes, members, capacity, slots_ref, counts_ref, q_ref, new_ref, cache_ref, out_ref,
    qbuf, kvbuf, acc, stat, part_out, part_in, stat_in,
    q_send, q_recv, kv_send, kv_recv, p_send, p_recv, s_send, s_recv,
):
    own = lax.axis_index("replica")
    plane, member = lax.div(own, members), lax.rem(own, members)
    heads_kv, lanes = acc.shape[1], acc.shape[3]
    tokens = lanes // PER_GROUP
    factor = HD ** (-0.5) * math.log2(math.e)
    square = members == 4
    last = members - 1

    def beside(way):
        return {"replica": lax.rem(plane + planes + 2 * way - 1, planes) * members + member}

    def in_plane(j):
        return {"replica": plane * members + plane_peer(member, j, members)}

    def back(j):
        return j if square else members - j

    def q_copy(way, origin):
        return pltpu.make_async_remote_copy(
            qbuf.at[origin], qbuf.at[origin], q_send.at[way, origin], q_recv.at[origin],
            device_id=beside(way), device_id_type=MESH)

    def kv_copy(j):
        return pltpu.make_async_remote_copy(
            cache_ref, kvbuf[back(j) - 1], kv_send.at[j], kv_recv.at[back(j)],
            device_id=in_plane(j), device_id_type=MESH)

    def corner_copy(half):
        via = kvbuf[1 - half]
        return pltpu.make_async_remote_copy(
            via.at[:, half], kvbuf[2].at[:, half], kv_send.at[3 + half], kv_recv.at[3 + half],
            device_id=in_plane(1 + half), device_id_type=MESH)

    def part_copy(way, target):
        return pltpu.make_async_remote_copy(
            part_out.at[target], part_in.at[way, target], p_send.at[target],
            p_recv.at[way, target],
            device_id=beside(way), device_id_type=MESH)

    def stat_copy(way, target):
        return pltpu.make_async_remote_copy(
            stat.at[target], stat_in.at[way, target], s_send.at[target], s_recv.at[way, target],
            device_id=beside(way), device_id_type=MESH)

    def has_next(way):
        return plane > 0 if way == 0 else plane < planes - 1

    barrier = pltpu.get_barrier_semaphore()
    for i in range(1, planes):
        column = {"replica": lax.rem(plane + i, planes) * members + member}
        pl.semaphore_signal(barrier, inc=1, device_id=column, device_id_type=MESH)
    for j in range(1, members):
        pl.semaphore_signal(barrier, inc=1, device_id=in_plane(j), device_id_type=MESH)
    for head in range(heads_kv * PER_GROUP):
        k, g = divmod(head, PER_GROUP)
        qbuf[plane, k, g * tokens:(g + 1) * tokens, :] = q_ref[:, head * HD:(head + 1) * HD]
    pl.semaphore_wait(barrier, planes + members - 2)

    for way in range(2):
        @pl.when(has_next(way))
        def _(way=way):
            q_copy(way, plane).start()
    for j in range(1, members - 1 if square else members):
        kv_copy(j).start()

    def update(i, k, keys, values, allowed):
        scores = lax.dot_general(
            keys, qbuf[i, k], (((1,), (1,)), ((), ())), preferred_element_type=jnp.float32)
        scores = jnp.where(allowed, scores * factor, MASKED)
        before = stat[i, k:k + 1, :]
        highest = jnp.maximum(before, jnp.max(scores, axis=0, keepdims=True))
        weights = jnp.exp2(scores - highest)
        scale = jnp.exp2(before - highest)
        total = stat[i, heads_kv + k:heads_kv + k + 1, :]
        stat[i, heads_kv + k:heads_kv + k + 1, :] = (
            total * scale + jnp.sum(weights, axis=0, keepdims=True))
        stat[i, k:k + 1, :] = highest
        acc[i, k] = acc[i, k] * scale + lax.dot_general(
            values, weights.astype(jnp.bfloat16), (((0,), (0,)), ((), ())),
            preferred_element_type=jnp.float32)

    def fold(i, j):
        source = cache_ref if j == 0 else kvbuf[j - 1]
        pair = i * members + j
        slots = [slots_ref[pair * capacity + c] for c in range(capacity)]
        rows = lax.broadcasted_iota(jnp.int32, (capacity * BLOCK, lanes), 0)
        allowed = rows < counts_ref[pair] * BLOCK
        for k in range(heads_kv):
            cut = slice(k * HD, (k + 1) * HD)
            keys = jnp.concatenate([source[s, 0, :, cut] for s in slots], axis=0)
            values = jnp.concatenate([source[s, 1, :, cut] for s in slots], axis=0)
            update(i, k, keys, values, allowed)

    def merge(way, i):
        for k in range(heads_kv):
            here, there = stat[i, k:k + 1, :], stat_in[way, i, k:k + 1, :]
            highest = jnp.maximum(here, there)
            mine, other = jnp.exp2(here - highest), jnp.exp2(there - highest)
            row = slice(heads_kv + k, heads_kv + k + 1)
            stat[i, row, :] = stat[i, row, :] * mine + stat_in[way, i, row, :] * other
            stat[i, k:k + 1, :] = highest
            acc[i, k] = acc[i, k] * mine + part_in[way, i, k].astype(jnp.float32) * other

    def clear(i, carry):
        acc[i] = jnp.zeros(acc.shape[1:], jnp.float32)
        stat[i, :heads_kv, :] = jnp.full((heads_kv, lanes), FLOOR, jnp.float32)
        stat[i, heads_kv:, :] = jnp.zeros((heads_kv, lanes), jnp.float32)
        return carry

    lax.fori_loop(0, planes, clear, 0)

    rows = lax.broadcasted_iota(jnp.int32, (tokens, lanes), 0)
    cols = lax.broadcasted_iota(jnp.int32, (tokens, lanes), 1)
    causal = rows <= cols % tokens
    for k in range(heads_kv):
        cut = slice(k * HD, (k + 1) * HD)
        update(plane, k, new_ref[0, :, cut], new_ref[1, :, cut], causal)
    fold(plane, 0)

    def pass_queries(distance):
        for way in range(2):
            origin = plane + distance * (1 - 2 * way)

            @pl.when((origin >= 0) & (origin < planes))
            def _(way=way, origin=origin):
                q_copy(way, origin).wait_recv()

                @pl.when(has_next(way))
                def _():
                    q_copy(way, origin).start()

    def near(distance, js):
        def side(t, carry):
            origin = plane + distance * (1 - 2 * t)

            @pl.when((origin >= 0) & (origin < planes))
            def _():
                for j in js:
                    fold(origin, j)
            return carry
        lax.fori_loop(0, 2, side, 0)

    early = range(1, last)
    pass_queries(1)
    near(1, (0,))
    for j in early:
        kv_copy(back(j)).wait_recv()
    if square:
        for half in range(2):
            corner_copy(half).start()
    pass_queries(2)

    def three(t, carry):
        origin = plane + t - 1

        @pl.when((origin >= 0) & (origin < planes))
        def _():
            for j in early:
                fold(origin, j)
        return carry

    lax.fori_loop(0, 3, three, 0)

    def far(distance, carry):
        @pl.when(distance > 2)
        def _():
            pass_queries(distance)
        near(distance, (0, *early))
        return carry

    lax.fori_loop(2, planes, far, 0)

    if square:
        for half in range(2):
            corner_copy(half).wait_recv()
    else:
        kv_copy(back(last)).wait_recv()

    def give(step, carry):
        for way in range(2):
            behind = planes - 1 - plane if way == 0 else plane
            rank = step - behind
            target = rank if way == 0 else planes - 1 - rank
            beyond = target < plane if way == 0 else target > plane

            @pl.when((rank >= 0) & beyond)
            def _(way=way, target=target, behind=behind):
                fold(target, last)

                @pl.when(behind > 0)
                def _():
                    part_copy(way, target).wait_recv()
                    stat_copy(way, target).wait_recv()
                    merge(way, target)
                part_out[target] = acc[target].astype(jnp.bfloat16)
                part_copy(way, target).start()
                stat_copy(way, target).start()
        return carry

    lax.fori_loop(0, planes - 1, give, 0)
    fold(plane, last)
    for way in range(2):
        @pl.when(has_next(1 - way))
        def _(way=way):
            part_copy(way, plane).wait_recv()
            stat_copy(way, plane).wait_recv()
            merge(way, plane)

    for k in range(heads_kv):
        mixed = acc[plane, k] / stat[plane, heads_kv + k:heads_kv + k + 1, :]
        for g in range(PER_GROUP):
            head = k * PER_GROUP + g
            tile = mixed[:, g * tokens:(g + 1) * tokens]
            out_ref[:, head * HD:(head + 1) * HD] = tile.T.astype(jnp.bfloat16)

    def sent(i, carry):
        for way in range(2):
            passed = i >= plane if way == 0 else i <= plane

            @pl.when(passed & has_next(way))
            def _(way=way):
                q_copy(way, i).wait_send()

        @pl.when(i != plane)
        def _():
            part_copy(0, i).wait_send()
            stat_copy(0, i).wait_send()
        return carry

    lax.fori_loop(0, planes, sent, 0)
    for j in range(1, members - 1 if square else members):
        kv_copy(j).wait_send()
    if square:
        for half in range(2):
            corner_copy(half).wait_send()


def local(queries, new_kv, cache, block_owner, block_slot, prefix_blocks, out_weight):
    replicas = lax.axis_size("replica")
    own = lax.axis_index("replica")
    capacity = max(2, MAXB // replicas)
    planes = math.isqrt(replicas)
    members = replicas // planes
    tokens, heads_kv = queries.shape[0], cache.shape[3] // HD
    lanes = PER_GROUP * tokens
    slots, counts = block_tables(
        block_owner, block_slot, prefix_blocks, own, planes, members, capacity)
    part = (planes, heads_kv, HD, lanes)
    stats = (planes, 2 * heads_kv, lanes)
    vmem = pl.BlockSpec(memory_space=pltpu.VMEM)
    smem = pl.BlockSpec(memory_space=pltpu.SMEM)
    pairs = replicas * capacity * BLOCK * heads_kv * lanes
    attended = pl.pallas_call(
        functools.partial(attend_kernel, planes, members, capacity),
        out_shape=jax.ShapeDtypeStruct(queries.shape, jnp.bfloat16),
        in_specs=[smem, smem, vmem, vmem, vmem],
        out_specs=vmem,
        scratch_shapes=[
            pltpu.VMEM((planes, heads_kv, lanes, HD), jnp.bfloat16),
            [pltpu.VMEM(cache.shape, jnp.bfloat16) for _ in range(members - 1)],
            pltpu.VMEM(part, jnp.float32),
            pltpu.VMEM(stats, jnp.float32),
            pltpu.VMEM(part, jnp.bfloat16),
            pltpu.VMEM((2, *part), jnp.bfloat16),
            pltpu.VMEM((2, *stats), jnp.float32),
            pltpu.SemaphoreType.DMA((2, planes)),
            pltpu.SemaphoreType.DMA((planes,)),
            pltpu.SemaphoreType.DMA((members + 1,)),
            pltpu.SemaphoreType.DMA((members + 1,)),
            pltpu.SemaphoreType.DMA((planes,)),
            pltpu.SemaphoreType.DMA((2, planes)),
            pltpu.SemaphoreType.DMA((planes,)),
            pltpu.SemaphoreType.DMA((2, planes)),
        ],
        compiler_params=pltpu.CompilerParams(
            collective_id=0, has_side_effects=True, vmem_limit_bytes=40 * 1024 * 1024),
        cost_estimate=pl.CostEstimate(
            flops=4 * pairs * HD, bytes_accessed=4 * cache.size, transcendentals=pairs),
    )(slots, counts, queries, new_kv, cache)
    return lax.psum_scatter(
        jnp.dot(attended, out_weight, preferred_element_type=jnp.float32).astype(jnp.bfloat16),
        "tensor",
        scatter_dimension=0,
        tiled=True,
    )


def solution(mesh):
    placed = (
        P("replica", "tensor"),
        P(None, "replica", "tensor"),
        P("replica", None, None, "tensor"),
        P(),
        P(),
        P(),
        P("tensor", None),
    )
    return jax.shard_map(
        local, mesh=mesh, in_specs=placed, out_specs=P(("replica", "tensor"), None), check_vma=False
    )
```

```python
import functools
import math

import jax
import jax.numpy as jnp
from jax import lax
from jax.experimental import pallas as pl
from jax.experimental.pallas import tpu as pltpu
from jax.sharding import PartitionSpec as P

HQ = 32
KVH = 8
HD = 128
BLOCK = 64
MAXB = 64
PER_GROUP = HQ // KVH

FLOOR = -1e29
MASKED = -2e30
MESH = pl.DeviceIdType.MESH


def block_tables(block_owner, block_slot, prefix_blocks, own, planes, members, capacity):
    plane, member = own // members, own % members
    owners = plane * members + jnp.stack(
        [plane_peer(member, j, members) for j in range(members)])
    places = jnp.arange(block_owner.shape[1], dtype=jnp.int32)
    owner_rows, slot_rows, lengths = [
        lax.dynamic_index_in_dim(
            table.reshape(planes, members, *table.shape[1:]), member, 1, keepdims=False)
        for table in (block_owner, block_slot, prefix_blocks)]
    used = places[None, :] < lengths[:, None]
    chosen = (owner_rows[:, None, :] == owners[None, :, None]) & used[:, None, :]
    earlier = places[None, :] < places[:, None]
    ranks = jnp.sum((chosen[:, :, None, :] & earlier).astype(jnp.int32), axis=3)
    levels = jnp.arange(capacity, dtype=jnp.int32)
    matches = chosen[:, :, None, :] & (ranks[:, :, None, :] == levels[None, None, :, None])
    slots = jnp.sum(jnp.where(matches, slot_rows[:, None, None, :], 0), axis=3)
    return slots.reshape(-1), jnp.sum(chosen.astype(jnp.int32), axis=2).reshape(-1)


def plane_peer(member, j, members):
    if members == 4:
        x, y = member % 2, member // 2
        return member + (j % 2) * (1 - 2 * x) + (j // 2) * (2 - 4 * y)
    return (member + j) % members


def attend_kernel(
    planes, members, capacity, slots_ref, counts_ref, q_hbm, new_hbm, cache_hbm, weight_hbm, out_ref,
    q_ref, new_ref, cache_ref, weight_ref, attended, mine, theirs, in_sem, y_send, y_recv,
    qbuf, kvbuf, acc, stat, part_out, part_in, stat_in,
    q_send, q_recv, kv_send, kv_recv, p_send, p_recv, s_send, s_recv,
):
    own = lax.axis_index("replica")
    plane, member = lax.div(own, members), lax.rem(own, members)
    heads_kv, lanes = acc.shape[1], acc.shape[3]
    tokens = lanes // PER_GROUP
    factor = HD ** (-0.5) * math.log2(math.e)
    square = members == 4
    last = members - 1

    def beside(way):
        return {"replica": lax.rem(plane + planes + 2 * way - 1, planes) * members + member}

    def in_plane(j):
        return {"replica": plane * members + plane_peer(member, j, members)}

    def back(j):
        return j if square else members - j

    def q_copy(way, origin):
        return pltpu.make_async_remote_copy(
            qbuf.at[origin], qbuf.at[origin], q_send.at[way, origin], q_recv.at[origin],
            device_id=beside(way), device_id_type=MESH)

    def kv_copy(j):
        return pltpu.make_async_remote_copy(
            cache_hbm, kvbuf[back(j) - 1], kv_send.at[j], kv_recv.at[back(j)],
            device_id=in_plane(j), device_id_type=MESH)

    def corner_copy(half):
        via = kvbuf[1 - half]
        return pltpu.make_async_remote_copy(
            via.at[:, half], kvbuf[2].at[:, half], kv_send.at[3 + half], kv_recv.at[3 + half],
            device_id=in_plane(1 + half), device_id_type=MESH)

    def part_copy(way, target):
        return pltpu.make_async_remote_copy(
            part_out.at[target], part_in.at[way, target], p_send.at[target],
            p_recv.at[way, target],
            device_id=beside(way), device_id_type=MESH)

    def stat_copy(way, target):
        return pltpu.make_async_remote_copy(
            stat.at[target], stat_in.at[way, target], s_send.at[target], s_recv.at[way, target],
            device_id=beside(way), device_id_type=MESH)

    def has_next(way):
        return plane > 0 if way == 0 else plane < planes - 1

    tensors, rank_t = lax.axis_size("tensor"), lax.axis_index("tensor")
    tiles, tile_rows, tile_cols = mine.shape[1:]

    def y_copy(k, tile):
        target = lax.rem(rank_t + k, tensors)
        return pltpu.make_async_remote_copy(
            mine.at[target, tile], theirs.at[tensors - k, tile],
            y_send.at[k, tile], y_recv.at[tensors - k, tile],
            device_id={"tensor": target}, device_id_type=MESH)

    loads = [
        pltpu.make_async_copy(source, place, in_sem.at[n]) for n, (source, place) in enumerate(
            ((q_hbm, q_ref), (new_hbm, new_ref), (cache_hbm, cache_ref), (weight_hbm, weight_ref)))]
    for load in loads[:3]:
        load.start()

    barrier = pltpu.get_barrier_semaphore()
    for k in range(1, tensors):
        pl.semaphore_signal(
            barrier, inc=1, device_id={"tensor": lax.rem(rank_t + k, tensors)}, device_id_type=MESH)
    for i in range(1, planes):
        column = {"replica": lax.rem(plane + i, planes) * members + member}
        pl.semaphore_signal(barrier, inc=1, device_id=column, device_id_type=MESH)
    for j in range(1, members):
        pl.semaphore_signal(barrier, inc=1, device_id=in_plane(j), device_id_type=MESH)
    loads[0].wait()
    for head in range(heads_kv * PER_GROUP):
        k, g = divmod(head, PER_GROUP)
        qbuf[plane, k, g * tokens:(g + 1) * tokens, :] = q_ref[:, head * HD:(head + 1) * HD]
    pl.semaphore_wait(barrier, planes + members + tensors - 3)

    for way in range(2):
        @pl.when(has_next(way))
        def _(way=way):
            q_copy(way, plane).start()
    for j in range(1, members - 1 if square else members):
        kv_copy(j).start()

    def update(i, k, keys, values, allowed):
        scores = lax.dot_general(
            keys, qbuf[i, k], (((1,), (1,)), ((), ())), preferred_element_type=jnp.float32)
        scores = jnp.where(allowed, scores * factor, MASKED)
        before = stat[i, k:k + 1, :]
        highest = jnp.maximum(before, jnp.max(scores, axis=0, keepdims=True))
        weights = jnp.exp2(scores - highest)
        scale = jnp.exp2(before - highest)
        total = stat[i, heads_kv + k:heads_kv + k + 1, :]
        stat[i, heads_kv + k:heads_kv + k + 1, :] = (
            total * scale + jnp.sum(weights, axis=0, keepdims=True))
        stat[i, k:k + 1, :] = highest
        acc[i, k] = acc[i, k] * scale + lax.dot_general(
            values, weights.astype(jnp.bfloat16), (((0,), (0,)), ((), ())),
            preferred_element_type=jnp.float32)

    def fold(i, j):
        source = cache_ref if j == 0 else kvbuf[j - 1]
        pair = i * members + j
        slots = [slots_ref[pair * capacity + c] for c in range(capacity)]
        rows = lax.broadcasted_iota(jnp.int32, (capacity * BLOCK, lanes), 0)
        allowed = rows < counts_ref[pair] * BLOCK
        for k in range(heads_kv):
            cut = slice(k * HD, (k + 1) * HD)
            keys = jnp.concatenate([source[s, 0, :, cut] for s in slots], axis=0)
            values = jnp.concatenate([source[s, 1, :, cut] for s in slots], axis=0)
            update(i, k, keys, values, allowed)

    def merge(way, i):
        for k in range(heads_kv):
            here, there = stat[i, k:k + 1, :], stat_in[way, i, k:k + 1, :]
            highest = jnp.maximum(here, there)
            mine, other = jnp.exp2(here - highest), jnp.exp2(there - highest)
            row = slice(heads_kv + k, heads_kv + k + 1)
            stat[i, row, :] = stat[i, row, :] * mine + stat_in[way, i, row, :] * other
            stat[i, k:k + 1, :] = highest
            acc[i, k] = acc[i, k] * mine + part_in[way, i, k].astype(jnp.float32) * other

    def clear(i, carry):
        acc[i] = jnp.zeros(acc.shape[1:], jnp.float32)
        stat[i, :heads_kv, :] = jnp.full((heads_kv, lanes), FLOOR, jnp.float32)
        stat[i, heads_kv:, :] = jnp.zeros((heads_kv, lanes), jnp.float32)
        return carry

    lax.fori_loop(0, planes, clear, 0)
    loads[3].start()
    loads[1].wait()
    loads[2].wait()

    rows = lax.broadcasted_iota(jnp.int32, (tokens, lanes), 0)
    cols = lax.broadcasted_iota(jnp.int32, (tokens, lanes), 1)
    causal = rows <= cols % tokens
    for k in range(heads_kv):
        cut = slice(k * HD, (k + 1) * HD)
        update(plane, k, new_ref[0, :, cut], new_ref[1, :, cut], causal)
    fold(plane, 0)

    def pass_queries(distance):
        for way in range(2):
            origin = plane + distance * (1 - 2 * way)

            @pl.when((origin >= 0) & (origin < planes))
            def _(way=way, origin=origin):
                q_copy(way, origin).wait_recv()

                @pl.when(has_next(way))
                def _():
                    q_copy(way, origin).start()

    def near(distance, js):
        def side(t, carry):
            origin = plane + distance * (1 - 2 * t)

            @pl.when((origin >= 0) & (origin < planes))
            def _():
                for j in js:
                    fold(origin, j)
            return carry
        lax.fori_loop(0, 2, side, 0)

    early = range(1, last)
    pass_queries(1)
    near(1, (0,))
    for j in early:
        kv_copy(back(j)).wait_recv()
    if square:
        for half in range(2):
            corner_copy(half).start()
    pass_queries(2)

    def three(t, carry):
        origin = plane + t - 1

        @pl.when((origin >= 0) & (origin < planes))
        def _():
            for j in early:
                fold(origin, j)
        return carry

    lax.fori_loop(0, 3, three, 0)

    def far(distance, carry):
        @pl.when(distance > 2)
        def _():
            pass_queries(distance)
        near(distance, (0, *early))
        return carry

    lax.fori_loop(2, planes, far, 0)

    if square:
        for half in range(2):
            corner_copy(half).wait_recv()
    else:
        kv_copy(back(last)).wait_recv()

    def give(step, carry):
        for way in range(2):
            behind = planes - 1 - plane if way == 0 else plane
            rank = step - behind
            target = rank if way == 0 else planes - 1 - rank
            beyond = target < plane if way == 0 else target > plane

            @pl.when((rank >= 0) & beyond)
            def _(way=way, target=target, behind=behind):
                fold(target, last)

                @pl.when(behind > 0)
                def _():
                    part_copy(way, target).wait_recv()
                    stat_copy(way, target).wait_recv()
                    merge(way, target)
                part_out[target] = acc[target].astype(jnp.bfloat16)
                part_copy(way, target).start()
                stat_copy(way, target).start()
        return carry

    lax.fori_loop(0, planes - 1, give, 0)
    fold(plane, last)
    for way in range(2):
        @pl.when(has_next(1 - way))
        def _(way=way):
            part_copy(way, plane).wait_recv()
            stat_copy(way, plane).wait_recv()
            merge(way, plane)

    for k in range(heads_kv):
        mixed = acc[plane, k] / stat[plane, heads_kv + k:heads_kv + k + 1, :]
        for g in range(PER_GROUP):
            head = k * PER_GROUP + g
            tile = mixed[:, g * tokens:(g + 1) * tokens]
            attended[:, head * HD:(head + 1) * HD] = tile.T.astype(jnp.bfloat16)

    loads[3].wait()

    def project(tile, carry):
        cols = pl.ds(pl.multiple_of(tile * tile_cols, tile_cols), tile_cols)
        product = jnp.dot(
            attended[...], weight_ref[:, cols], preferred_element_type=jnp.float32)
        product = product.astype(jnp.bfloat16)
        for t in range(tensors):
            mine[t, tile] = product[t * tile_rows:(t + 1) * tile_rows]
        for k in range(1, tensors):
            y_copy(k, tile).start()
        return carry

    lax.fori_loop(0, tiles, project, 0)

    def add_up(tile, carry):
        cols = pl.ds(pl.multiple_of(tile * tile_cols, tile_cols), tile_cols)
        total = mine[rank_t, tile].astype(jnp.float32)
        for k in range(1, tensors):
            y_copy(tensors - k, tile).wait_recv()
            total += theirs[k, tile].astype(jnp.float32)
        out_ref[:, cols] = total.astype(jnp.bfloat16)
        for k in range(1, tensors):
            y_copy(k, tile).wait_send()
        return carry

    lax.fori_loop(0, tiles, add_up, 0)

    def sent(i, carry):
        for way in range(2):
            passed = i >= plane if way == 0 else i <= plane

            @pl.when(passed & has_next(way))
            def _(way=way):
                q_copy(way, i).wait_send()

        @pl.when(i != plane)
        def _():
            part_copy(0, i).wait_send()
            stat_copy(0, i).wait_send()
        return carry

    lax.fori_loop(0, planes, sent, 0)
    for j in range(1, members - 1 if square else members):
        kv_copy(j).wait_send()
    if square:
        for half in range(2):
            corner_copy(half).wait_send()


def local(queries, new_kv, cache, block_owner, block_slot, prefix_blocks, out_weight):
    replicas = lax.axis_size("replica")
    own = lax.axis_index("replica")
    capacity = max(2, MAXB // replicas)
    planes = math.isqrt(replicas)
    members = replicas // planes
    tokens, heads_kv = queries.shape[0], cache.shape[3] // HD
    lanes = PER_GROUP * tokens
    slots, counts = block_tables(
        block_owner, block_slot, prefix_blocks, own, planes, members, capacity)
    part = (planes, heads_kv, HD, lanes)
    stats = (planes, 2 * heads_kv, lanes)
    vmem = pl.BlockSpec(memory_space=pltpu.VMEM)
    smem = pl.BlockSpec(memory_space=pltpu.SMEM)
    pairs = replicas * capacity * BLOCK * heads_kv * lanes
    tensors, width = lax.axis_size("tensor"), out_weight.shape[1]
    tile_cols = min(512, width)
    halves = (tensors, width // tile_cols, tokens // tensors, tile_cols)
    anywhere = pl.BlockSpec(memory_space=pl.ANY)
    return pl.pallas_call(
        functools.partial(attend_kernel, planes, members, capacity),
        out_shape=jax.ShapeDtypeStruct((tokens // tensors, width), jnp.bfloat16),
        in_specs=[smem, smem, anywhere, anywhere, anywhere, anywhere],
        out_specs=vmem,
        scratch_shapes=[
            *[pltpu.VMEM(a.shape, jnp.bfloat16) for a in (queries, new_kv, cache, out_weight)],
            pltpu.VMEM(queries.shape, jnp.bfloat16),
            pltpu.VMEM(halves, jnp.bfloat16),
            pltpu.VMEM(halves, jnp.bfloat16),
            pltpu.SemaphoreType.DMA((4,)),
            pltpu.SemaphoreType.DMA(halves[:2]),
            pltpu.SemaphoreType.DMA(halves[:2]),
            pltpu.VMEM((planes, heads_kv, lanes, HD), jnp.bfloat16),
            [pltpu.VMEM(cache.shape, jnp.bfloat16) for _ in range(members - 1)],
            pltpu.VMEM(part, jnp.float32),
            pltpu.VMEM(stats, jnp.float32),
            pltpu.VMEM(part, jnp.bfloat16),
            pltpu.VMEM((2, *part), jnp.bfloat16),
            pltpu.VMEM((2, *stats), jnp.float32),
            pltpu.SemaphoreType.DMA((2, planes)),
            pltpu.SemaphoreType.DMA((planes,)),
            pltpu.SemaphoreType.DMA((members + 1,)),
            pltpu.SemaphoreType.DMA((members + 1,)),
            pltpu.SemaphoreType.DMA((planes,)),
            pltpu.SemaphoreType.DMA((2, planes)),
            pltpu.SemaphoreType.DMA((planes,)),
            pltpu.SemaphoreType.DMA((2, planes)),
        ],
        compiler_params=pltpu.CompilerParams(
            collective_id=0, has_side_effects=True, vmem_limit_bytes=56 * 1024 * 1024),
        cost_estimate=pl.CostEstimate(
            flops=4 * pairs * HD, bytes_accessed=4 * cache.size + 2 * out_weight.size, transcendentals=pairs),
    )(slots, counts, queries, new_kv, cache, out_weight)


def solution(mesh):
    placed = (
        P("replica", "tensor"),
        P(None, "replica", "tensor"),
        P("replica", None, None, "tensor"),
        P(),
        P(),
        P(),
        P("tensor", None),
    )
    return jax.shard_map(
        local, mesh=mesh, in_specs=placed, out_specs=P(("replica", "tensor"), None), check_vma=False
    )
```

```python
import functools
import math

import jax
import jax.numpy as jnp
from jax import lax
from jax.experimental import pallas as pl
from jax.experimental.pallas import tpu as pltpu
from jax.sharding import PartitionSpec as P

HQ = 32
KVH = 8
HD = 128
BLOCK = 64
MAXB = 64
PER_GROUP = HQ // KVH

FLOOR = -1e29
MASKED = -2e30
MESH = pl.DeviceIdType.MESH


def block_tables(block_owner, block_slot, prefix_blocks, own, planes, members, capacity):
    plane, member = own // members, own % members
    owners = plane * members + jnp.stack(
        [plane_peer(member, j, members) for j in range(members)])
    places = jnp.arange(block_owner.shape[1], dtype=jnp.int32)
    owner_rows, slot_rows, lengths = [
        lax.dynamic_index_in_dim(
            table.reshape(planes, members, *table.shape[1:]), member, 1, keepdims=False)
        for table in (block_owner, block_slot, prefix_blocks)]
    used = places[None, :] < lengths[:, None]
    chosen = (owner_rows[:, None, :] == owners[None, :, None]) & used[:, None, :]
    earlier = places[None, :] < places[:, None]
    ranks = jnp.sum((chosen[:, :, None, :] & earlier).astype(jnp.int32), axis=3)
    levels = jnp.arange(capacity, dtype=jnp.int32)
    matches = chosen[:, :, None, :] & (ranks[:, :, None, :] == levels[None, None, :, None])
    slots = jnp.sum(jnp.where(matches, slot_rows[:, None, None, :], 0), axis=3)
    return slots.reshape(-1), jnp.sum(chosen.astype(jnp.int32), axis=2).reshape(-1)


def plane_peer(member, j, members):
    if members == 4:
        x, y = member % 2, member // 2
        return member + (j % 2) * (1 - 2 * x) + (j // 2) * (2 - 4 * y)
    return (member + j) % members


def attend_kernel(
    planes, members, capacity, slots_ref, counts_ref, q_hbm, new_hbm, cache_hbm, weight_hbm, out_ref,
    q_ref, new_ref, cache_ref, weight_ref, attended, mine, theirs, in_sem, y_send, y_recv,
    qbuf, kvbuf, acc, stat, part_out, part_in, stat_in,
    q_send, q_recv, kv_send, kv_recv, p_send, p_recv, s_send, s_recv,
):
    own = lax.axis_index("replica")
    plane, member = lax.div(own, members), lax.rem(own, members)
    heads_kv, lanes = acc.shape[1], acc.shape[3]
    tokens = lanes // PER_GROUP
    factor = HD ** (-0.5) * math.log2(math.e)
    square = members == 4
    last = members - 1

    def beside(way):
        return {"replica": lax.rem(plane + planes + 2 * way - 1, planes) * members + member}

    def in_plane(j):
        return {"replica": plane * members + plane_peer(member, j, members)}

    def back(j):
        return j if square else members - j

    def q_copy(way, origin):
        return pltpu.make_async_remote_copy(
            qbuf.at[origin], qbuf.at[origin], q_send.at[way, origin], q_recv.at[origin],
            device_id=beside(way), device_id_type=MESH)

    def kv_copy(j):
        return pltpu.make_async_remote_copy(
            cache_hbm, kvbuf[back(j) - 1], kv_send.at[j], kv_recv.at[back(j)],
            device_id=in_plane(j), device_id_type=MESH)

    def corner_copy(half):
        via = kvbuf[1 - half]
        return pltpu.make_async_remote_copy(
            via.at[:, half], kvbuf[2].at[:, half], kv_send.at[3 + half], kv_recv.at[3 + half],
            device_id=in_plane(1 + half), device_id_type=MESH)

    def part_copy(way, target, k):
        return pltpu.make_async_remote_copy(
            part_out.at[target, k], part_in.at[way, target, k], p_send.at[target, k],
            p_recv.at[way, target, k],
            device_id=beside(way), device_id_type=MESH)

    def stat_copy(way, target, k):
        return pltpu.make_async_remote_copy(
            stat.at[target, k], stat_in.at[way, target, k], s_send.at[target, k],
            s_recv.at[way, target, k],
            device_id=beside(way), device_id_type=MESH)

    def has_next(way):
        return plane > 0 if way == 0 else plane < planes - 1

    tensors, rank_t = lax.axis_size("tensor"), lax.axis_index("tensor")
    tiles, tile_rows, tile_cols = mine.shape[1:]

    def y_copy(k, tile):
        target = lax.rem(rank_t + k, tensors)
        return pltpu.make_async_remote_copy(
            mine.at[target, tile], theirs.at[tensors - k, tile],
            y_send.at[k, tile], y_recv.at[tensors - k, tile],
            device_id={"tensor": target}, device_id_type=MESH)

    loads = [
        pltpu.make_async_copy(source, place, in_sem.at[n]) for n, (source, place) in enumerate(
            ((q_hbm, q_ref), (new_hbm, new_ref), (cache_hbm, cache_ref), (weight_hbm, weight_ref)))]
    for load in loads[:3]:
        load.start()

    barrier = pltpu.get_barrier_semaphore()
    for k in range(1, tensors):
        pl.semaphore_signal(
            barrier, inc=1, device_id={"tensor": lax.rem(rank_t + k, tensors)}, device_id_type=MESH)
    for i in range(1, planes):
        column = {"replica": lax.rem(plane + i, planes) * members + member}
        pl.semaphore_signal(barrier, inc=1, device_id=column, device_id_type=MESH)
    for j in range(1, members):
        pl.semaphore_signal(barrier, inc=1, device_id=in_plane(j), device_id_type=MESH)
    loads[0].wait()
    for head in range(heads_kv * PER_GROUP):
        k, g = divmod(head, PER_GROUP)
        qbuf[plane, k, g * tokens:(g + 1) * tokens, :] = q_ref[:, head * HD:(head + 1) * HD]
    pl.semaphore_wait(barrier, planes + members + tensors - 3)

    for way in range(2):
        @pl.when(has_next(way))
        def _(way=way):
            q_copy(way, plane).start()
    for j in range(1, members - 1 if square else members):
        kv_copy(j).start()

    def update(i, k, keys, values, allowed):
        scores = lax.dot_general(
            keys, qbuf[i, k], (((1,), (1,)), ((), ())), preferred_element_type=jnp.float32)
        scores = jnp.where(allowed, scores * factor, MASKED)
        before = stat[i, k, :1, :]
        highest = jnp.maximum(before, jnp.max(scores, axis=0, keepdims=True))
        weights = jnp.exp2(scores - highest)
        scale = jnp.exp2(before - highest)
        total = stat[i, k, 1:, :]
        stat[i, k, 1:, :] = (
            total * scale + jnp.sum(weights, axis=0, keepdims=True))
        stat[i, k, :1, :] = highest
        acc[i, k] = acc[i, k] * scale + lax.dot_general(
            values, weights.astype(jnp.bfloat16), (((0,), (0,)), ((), ())),
            preferred_element_type=jnp.float32)

    def fold(i, j, heads=range(heads_kv)):
        source = cache_ref if j == 0 else kvbuf[j - 1]
        pair = i * members + j
        slots = [slots_ref[pair * capacity + c] for c in range(capacity)]
        rows = lax.broadcasted_iota(jnp.int32, (capacity * BLOCK, lanes), 0)
        allowed = rows < counts_ref[pair] * BLOCK
        for k in heads:
            cut = slice(k * HD, (k + 1) * HD)
            keys = jnp.concatenate([source[s, 0, :, cut] for s in slots], axis=0)
            values = jnp.concatenate([source[s, 1, :, cut] for s in slots], axis=0)
            update(i, k, keys, values, allowed)

    def merge(way, i, k):
        part_copy(way, i, k).wait_recv()
        stat_copy(way, i, k).wait_recv()
        here, there = stat[i, k, :1, :], stat_in[way, i, k, :1, :]
        highest = jnp.maximum(here, there)
        mine, other = jnp.exp2(here - highest), jnp.exp2(there - highest)
        stat[i, k, 1:, :] = stat[i, k, 1:, :] * mine + stat_in[way, i, k, 1:, :] * other
        stat[i, k, :1, :] = highest
        acc[i, k] = acc[i, k] * mine + part_in[way, i, k].astype(jnp.float32) * other

    def clear(i, carry):
        acc[i] = jnp.zeros(acc.shape[1:], jnp.float32)
        for k in range(heads_kv):
            stat[i, k, :1, :] = jnp.full((1, lanes), FLOOR, jnp.float32)
            stat[i, k, 1:, :] = jnp.zeros((1, lanes), jnp.float32)
        return carry

    lax.fori_loop(0, planes, clear, 0)
    loads[3].start()
    loads[1].wait()
    loads[2].wait()

    rows = lax.broadcasted_iota(jnp.int32, (tokens, lanes), 0)
    cols = lax.broadcasted_iota(jnp.int32, (tokens, lanes), 1)
    causal = rows <= cols % tokens
    for k in range(heads_kv):
        cut = slice(k * HD, (k + 1) * HD)
        update(plane, k, new_ref[0, :, cut], new_ref[1, :, cut], causal)
    fold(plane, 0)

    def pass_queries(distance):
        for way in range(2):
            origin = plane + distance * (1 - 2 * way)

            @pl.when((origin >= 0) & (origin < planes))
            def _(way=way, origin=origin):
                q_copy(way, origin).wait_recv()

                @pl.when(has_next(way))
                def _():
                    q_copy(way, origin).start()

    def near(distance, js):
        def side(t, carry):
            origin = plane + distance * (1 - 2 * t)

            @pl.when((origin >= 0) & (origin < planes))
            def _():
                for j in js:
                    fold(origin, j)
            return carry
        lax.fori_loop(0, 2, side, 0)

    early = range(1, last)
    pass_queries(1)
    near(1, (0,))
    for j in early:
        kv_copy(back(j)).wait_recv()
    if square:
        for half in range(2):
            corner_copy(half).start()
    pass_queries(2)

    def three(t, carry):
        origin = plane + t - 1

        @pl.when((origin >= 0) & (origin < planes))
        def _():
            for j in early:
                fold(origin, j)
        return carry

    lax.fori_loop(0, 3, three, 0)

    def far(distance, carry):
        @pl.when(distance > 2)
        def _():
            pass_queries(distance)
        near(distance, (0, *early))
        return carry

    lax.fori_loop(2, planes, far, 0)

    if square:
        for half in range(2):
            corner_copy(half).wait_recv()
    else:
        kv_copy(back(last)).wait_recv()

    def give(step, carry):
        for way in range(2):
            behind = planes - 1 - plane if way == 0 else plane
            rank = step - behind
            target = rank if way == 0 else planes - 1 - rank
            beyond = target < plane if way == 0 else target > plane

            @pl.when((rank >= 0) & beyond)
            def _(way=way, target=target, behind=behind):
                for k in range(heads_kv):
                    fold(target, last, (k,))

                    @pl.when(behind > 0)
                    def _(k=k):
                        merge(way, target, k)
                    part_out[target, k] = acc[target, k].astype(jnp.bfloat16)
                    part_copy(way, target, k).start()
                    stat_copy(way, target, k).start()
        return carry

    lax.fori_loop(0, planes - 1, give, 0)
    fold(plane, last)
    for way in range(2):
        @pl.when(has_next(1 - way))
        def _(way=way):
            for k in range(heads_kv):
                merge(way, plane, k)

    for k in range(heads_kv):
        mixed = acc[plane, k] / stat[plane, k, 1:, :]
        for g in range(PER_GROUP):
            head = k * PER_GROUP + g
            tile = mixed[:, g * tokens:(g + 1) * tokens]
            attended[:, head * HD:(head + 1) * HD] = tile.T.astype(jnp.bfloat16)

    loads[3].wait()

    def project(tile, carry):
        cols = pl.ds(pl.multiple_of(tile * tile_cols, tile_cols), tile_cols)
        product = jnp.dot(
            attended[...], weight_ref[:, cols], preferred_element_type=jnp.float32)
        product = product.astype(jnp.bfloat16)
        for t in range(tensors):
            mine[t, tile] = product[t * tile_rows:(t + 1) * tile_rows]
        for k in range(1, tensors):
            y_copy(k, tile).start()
        return carry

    lax.fori_loop(0, tiles, project, 0)

    def add_up(tile, carry):
        cols = pl.ds(pl.multiple_of(tile * tile_cols, tile_cols), tile_cols)
        total = mine[rank_t, tile].astype(jnp.float32)
        for k in range(1, tensors):
            y_copy(tensors - k, tile).wait_recv()
            total += theirs[k, tile].astype(jnp.float32)
        out_ref[:, cols] = total.astype(jnp.bfloat16)
        for k in range(1, tensors):
            y_copy(k, tile).wait_send()
        return carry

    lax.fori_loop(0, tiles, add_up, 0)

    def sent(i, carry):
        for way in range(2):
            passed = i >= plane if way == 0 else i <= plane

            @pl.when(passed & has_next(way))
            def _(way=way):
                q_copy(way, i).wait_send()

        @pl.when(i != plane)
        def _():
            for k in range(heads_kv):
                part_copy(0, i, k).wait_send()
                stat_copy(0, i, k).wait_send()
        return carry

    lax.fori_loop(0, planes, sent, 0)
    for j in range(1, members - 1 if square else members):
        kv_copy(j).wait_send()
    if square:
        for half in range(2):
            corner_copy(half).wait_send()


def local(queries, new_kv, cache, block_owner, block_slot, prefix_blocks, out_weight):
    replicas = lax.axis_size("replica")
    own = lax.axis_index("replica")
    capacity = max(2, MAXB // replicas)
    planes = math.isqrt(replicas)
    members = replicas // planes
    tokens, heads_kv = queries.shape[0], cache.shape[3] // HD
    lanes = PER_GROUP * tokens
    slots, counts = block_tables(
        block_owner, block_slot, prefix_blocks, own, planes, members, capacity)
    part = (planes, heads_kv, HD, lanes)
    stats = (planes, heads_kv, 2, lanes)
    vmem = pl.BlockSpec(memory_space=pltpu.VMEM)
    smem = pl.BlockSpec(memory_space=pltpu.SMEM)
    pairs = replicas * capacity * BLOCK * heads_kv * lanes
    tensors, width = lax.axis_size("tensor"), out_weight.shape[1]
    tile_cols = min(512, width)
    halves = (tensors, width // tile_cols, tokens // tensors, tile_cols)
    anywhere = pl.BlockSpec(memory_space=pl.ANY)
    return pl.pallas_call(
        functools.partial(attend_kernel, planes, members, capacity),
        out_shape=jax.ShapeDtypeStruct((tokens // tensors, width), jnp.bfloat16),
        in_specs=[smem, smem, anywhere, anywhere, anywhere, anywhere],
        out_specs=vmem,
        scratch_shapes=[
            *[pltpu.VMEM(a.shape, jnp.bfloat16) for a in (queries, new_kv, cache, out_weight)],
            pltpu.VMEM(queries.shape, jnp.bfloat16),
            pltpu.VMEM(halves, jnp.bfloat16),
            pltpu.VMEM(halves, jnp.bfloat16),
            pltpu.SemaphoreType.DMA((4,)),
            pltpu.SemaphoreType.DMA(halves[:2]),
            pltpu.SemaphoreType.DMA(halves[:2]),
            pltpu.VMEM((planes, heads_kv, lanes, HD), jnp.bfloat16),
            [pltpu.VMEM(cache.shape, jnp.bfloat16) for _ in range(members - 1)],
            pltpu.VMEM(part, jnp.float32),
            pltpu.VMEM(stats, jnp.float32),
            pltpu.VMEM(part, jnp.bfloat16),
            pltpu.VMEM((2, *part), jnp.bfloat16),
            pltpu.VMEM((2, *stats), jnp.float32),
            pltpu.SemaphoreType.DMA((2, planes)),
            pltpu.SemaphoreType.DMA((planes,)),
            pltpu.SemaphoreType.DMA((members + 1,)),
            pltpu.SemaphoreType.DMA((members + 1,)),
            pltpu.SemaphoreType.DMA((planes, heads_kv)),
            pltpu.SemaphoreType.DMA((2, planes, heads_kv)),
            pltpu.SemaphoreType.DMA((planes, heads_kv)),
            pltpu.SemaphoreType.DMA((2, planes, heads_kv)),
        ],
        compiler_params=pltpu.CompilerParams(
            collective_id=0, has_side_effects=True, vmem_limit_bytes=56 * 1024 * 1024),
        cost_estimate=pl.CostEstimate(
            flops=4 * pairs * HD, bytes_accessed=4 * cache.size + 2 * out_weight.size, transcendentals=pairs),
    )(slots, counts, queries, new_kv, cache, out_weight)


def solution(mesh):
    placed = (
        P("replica", "tensor"),
        P(None, "replica", "tensor"),
        P("replica", None, None, "tensor"),
        P(),
        P(),
        P(),
        P("tensor", None),
    )
    return jax.shard_map(
        local, mesh=mesh, in_specs=placed, out_specs=P(("replica", "tensor"), None), check_vma=False
    )
```

```python
import functools
import math

import jax
import jax.numpy as jnp
from jax import lax
from jax.experimental import pallas as pl
from jax.experimental.pallas import tpu as pltpu
from jax.sharding import PartitionSpec as P

HQ = 32
KVH = 8
HD = 128
BLOCK = 64
MAXB = 64
PER_GROUP = HQ // KVH

FLOOR = -1e29
MASKED = -2e30
MESH = pl.DeviceIdType.MESH


def block_tables(block_owner, block_slot, prefix_blocks, own, planes, members, capacity):
    plane, member = own // members, own % members
    owners = plane * members + jnp.stack(
        [plane_peer(member, j, members) for j in range(members)])
    places = jnp.arange(block_owner.shape[1], dtype=jnp.int32)
    owner_rows, slot_rows, lengths = [
        lax.dynamic_index_in_dim(
            table.reshape(planes, members, *table.shape[1:]), member, 1, keepdims=False)
        for table in (block_owner, block_slot, prefix_blocks)]
    used = places[None, :] < lengths[:, None]
    chosen = (owner_rows[:, None, :] == owners[None, :, None]) & used[:, None, :]
    earlier = places[None, :] < places[:, None]
    ranks = jnp.sum((chosen[:, :, None, :] & earlier).astype(jnp.int32), axis=3)
    levels = jnp.arange(capacity, dtype=jnp.int32)
    matches = chosen[:, :, None, :] & (ranks[:, :, None, :] == levels[None, None, :, None])
    slots = jnp.sum(jnp.where(matches, slot_rows[:, None, None, :], 0), axis=3)
    return slots.reshape(-1), jnp.sum(chosen.astype(jnp.int32), axis=2).reshape(-1)


def plane_peer(member, j, members):
    if members == 4:
        x, y = member % 2, member // 2
        return member + (j % 2) * (1 - 2 * x) + (j // 2) * (2 - 4 * y)
    return (member + j) % members


def attend_kernel(
    planes, members, capacity, slots_ref, counts_ref, q_hbm, new_hbm, cache_hbm, weight_hbm, out_ref,
    q_ref, new_ref, cache_ref, weight_ref, attended, mine, theirs, in_sem, y_send, y_recv,
    qbuf, kvbuf, acc, stat, part_out, part_in, stat_in,
    q_send, q_recv, kv_send, kv_recv, p_send, p_recv, s_send, s_recv,
):
    own = lax.axis_index("replica")
    plane, member = lax.div(own, members), lax.rem(own, members)
    heads_kv, lanes = acc.shape[1], acc.shape[3]
    tokens = lanes // PER_GROUP
    factor = HD ** (-0.5) * math.log2(math.e)
    square = members == 4
    last = members - 1

    def beside(way):
        return {"replica": lax.rem(plane + planes + 2 * way - 1, planes) * members + member}

    def in_plane(j):
        return {"replica": plane * members + plane_peer(member, j, members)}

    def back(j):
        return j if square else members - j

    def q_copy(way, origin):
        return pltpu.make_async_remote_copy(
            qbuf.at[origin], qbuf.at[origin], q_send.at[way, origin], q_recv.at[origin],
            device_id=beside(way), device_id_type=MESH)

    def kv_copy(j):
        return pltpu.make_async_remote_copy(
            cache_hbm, kvbuf[back(j) - 1], kv_send.at[j], kv_recv.at[back(j)],
            device_id=in_plane(j), device_id_type=MESH)

    def corner_copy(half):
        via = kvbuf[1 - half]
        return pltpu.make_async_remote_copy(
            via.at[:, half], kvbuf[2].at[:, half], kv_send.at[3 + half], kv_recv.at[3 + half],
            device_id=in_plane(1 + half), device_id_type=MESH)

    def part_copy(way, target, k):
        return pltpu.make_async_remote_copy(
            part_out.at[target, k], part_in.at[way, target, k], p_send.at[target, k],
            p_recv.at[way, target, k],
            device_id=beside(way), device_id_type=MESH)

    def stat_copy(way, target, k):
        return pltpu.make_async_remote_copy(
            stat.at[target, k], stat_in.at[way, target, k], s_send.at[target, k],
            s_recv.at[way, target, k],
            device_id=beside(way), device_id_type=MESH)

    def has_next(way):
        return plane > 0 if way == 0 else plane < planes - 1

    tensors, rank_t = lax.axis_size("tensor"), lax.axis_index("tensor")
    tiles, tile_rows, tile_cols = mine.shape[1:]

    def y_copy(k, tile):
        target = lax.rem(rank_t + k, tensors)
        return pltpu.make_async_remote_copy(
            mine.at[target, tile], theirs.at[tensors - k, tile],
            y_send.at[k, tile], y_recv.at[tensors - k, tile],
            device_id={"tensor": target}, device_id_type=MESH)

    loads = [
        pltpu.make_async_copy(source, place, in_sem.at[n]) for n, (source, place) in enumerate(
            ((q_hbm, q_ref), (new_hbm, new_ref), (cache_hbm, cache_ref), (weight_hbm, weight_ref)))]
    for load in loads[:3]:
        load.start()

    barrier = pltpu.get_barrier_semaphore()
    for k in range(1, tensors):
        pl.semaphore_signal(
            barrier, inc=1, device_id={"tensor": lax.rem(rank_t + k, tensors)}, device_id_type=MESH)
    for i in range(1, planes):
        column = {"replica": lax.rem(plane + i, planes) * members + member}
        pl.semaphore_signal(barrier, inc=1, device_id=column, device_id_type=MESH)
    for j in range(1, members):
        pl.semaphore_signal(barrier, inc=1, device_id=in_plane(j), device_id_type=MESH)
    loads[0].wait()
    for head in range(heads_kv * PER_GROUP):
        k, g = divmod(head, PER_GROUP)
        qbuf[plane, k, g * tokens:(g + 1) * tokens, :] = q_ref[:, head * HD:(head + 1) * HD]
    pl.semaphore_wait(barrier, planes + members + tensors - 3)

    for way in range(2):
        @pl.when(has_next(way))
        def _(way=way):
            q_copy(way, plane).start()
    for j in range(1, members - 1 if square else members):
        kv_copy(j).start()

    def update(i, k, keys, values, allowed):
        scores = lax.dot_general(
            keys, qbuf[i, k], (((1,), (1,)), ((), ())), preferred_element_type=jnp.float32)
        scores = jnp.where(allowed, scores * factor, MASKED)
        before = stat[i, k, :1, :]
        highest = jnp.maximum(before, jnp.max(scores, axis=0, keepdims=True))
        weights = jnp.exp2(scores - highest)
        scale = jnp.exp2(before - highest)
        total = stat[i, k, 1:, :]
        stat[i, k, 1:, :] = (
            total * scale + jnp.sum(weights, axis=0, keepdims=True))
        stat[i, k, :1, :] = highest
        acc[i, k] = acc[i, k] * scale + lax.dot_general(
            values, weights.astype(jnp.bfloat16), (((0,), (0,)), ((), ())),
            preferred_element_type=jnp.float32)

    def fold(i, j, heads=range(heads_kv)):
        source = cache_ref if j == 0 else kvbuf[j - 1]
        pair = i * members + j
        slots = [slots_ref[pair * capacity + c] for c in range(capacity)]
        rows = lax.broadcasted_iota(jnp.int32, (capacity * BLOCK, lanes), 0)
        allowed = rows < counts_ref[pair] * BLOCK
        for k in heads:
            cut = slice(k * HD, (k + 1) * HD)
            keys = jnp.concatenate([source[s, 0, :, cut] for s in slots], axis=0)
            values = jnp.concatenate([source[s, 1, :, cut] for s in slots], axis=0)
            update(i, k, keys, values, allowed)

    def merge(way, i, k):
        part_copy(way, i, k).wait_recv()
        stat_copy(way, i, k).wait_recv()
        here, there = stat[i, k, :1, :], stat_in[way, i, k, :1, :]
        highest = jnp.maximum(here, there)
        mine, other = jnp.exp2(here - highest), jnp.exp2(there - highest)
        stat[i, k, 1:, :] = stat[i, k, 1:, :] * mine + stat_in[way, i, k, 1:, :] * other
        stat[i, k, :1, :] = highest
        acc[i, k] = acc[i, k] * mine + part_in[way, i, k].astype(jnp.float32) * other

    def clear(i, carry):
        acc[i] = jnp.zeros(acc.shape[1:], jnp.float32)
        for k in range(heads_kv):
            stat[i, k, :1, :] = jnp.full((1, lanes), FLOOR, jnp.float32)
            stat[i, k, 1:, :] = jnp.zeros((1, lanes), jnp.float32)
        return carry

    lax.fori_loop(0, planes, clear, 0)
    loads[3].start()
    loads[1].wait()
    loads[2].wait()

    rows = lax.broadcasted_iota(jnp.int32, (tokens, lanes), 0)
    cols = lax.broadcasted_iota(jnp.int32, (tokens, lanes), 1)
    causal = rows <= cols % tokens
    for k in range(heads_kv):
        cut = slice(k * HD, (k + 1) * HD)
        update(plane, k, new_ref[0, :, cut], new_ref[1, :, cut], causal)
    fold(plane, 0)

    def pass_queries(distance):
        for way in range(2):
            origin = plane + distance * (1 - 2 * way)

            @pl.when((origin >= 0) & (origin < planes))
            def _(way=way, origin=origin):
                q_copy(way, origin).wait_recv()

                @pl.when(has_next(way))
                def _():
                    q_copy(way, origin).start()

    def near(distance, js):
        def side(t, carry):
            origin = plane + distance * (1 - 2 * t)

            @pl.when((origin >= 0) & (origin < planes))
            def _():
                for j in js:
                    fold(origin, j)
            return carry
        lax.fori_loop(0, 2, side, 0)

    early = range(1, last)
    pass_queries(1)
    near(1, (0,))
    for j in early:
        kv_copy(back(j)).wait_recv()
    if square:
        for half in range(2):
            corner_copy(half).start()
    pass_queries(2)

    near(1, early)

    def far(distance, carry):
        @pl.when(distance > 2)
        def _():
            pass_queries(distance)
        near(distance, (0, *early))
        return carry

    lax.fori_loop(2, planes, far, 0)

    if square:
        for half in range(2):
            corner_copy(half).wait_recv()
    else:
        kv_copy(back(last)).wait_recv()

    def give(step, carry):
        for way in range(2):
            behind = planes - 1 - plane if way == 0 else plane
            rank = step - behind
            target = rank if way == 0 else planes - 1 - rank
            beyond = target < plane if way == 0 else target > plane

            @pl.when((rank >= 0) & beyond)
            def _(way=way, target=target, behind=behind):
                for k in range(heads_kv):
                    fold(target, last, (k,))

                    @pl.when(behind > 0)
                    def _(k=k):
                        merge(way, target, k)
                    part_out[target, k] = acc[target, k].astype(jnp.bfloat16)
                    part_copy(way, target, k).start()
                    stat_copy(way, target, k).start()
        return carry

    lax.fori_loop(0, planes - 1, give, 0)
    for j in (*early, last):
        fold(plane, j)
    for way in range(2):
        @pl.when(has_next(1 - way))
        def _(way=way):
            for k in range(heads_kv):
                merge(way, plane, k)

    for k in range(heads_kv):
        mixed = acc[plane, k] / stat[plane, k, 1:, :]
        for g in range(PER_GROUP):
            head = k * PER_GROUP + g
            tile = mixed[:, g * tokens:(g + 1) * tokens]
            attended[:, head * HD:(head + 1) * HD] = tile.T.astype(jnp.bfloat16)

    loads[3].wait()

    def project(tile, carry):
        cols = pl.ds(pl.multiple_of(tile * tile_cols, tile_cols), tile_cols)
        product = jnp.dot(
            attended[...], weight_ref[:, cols], preferred_element_type=jnp.float32)
        product = product.astype(jnp.bfloat16)
        for t in range(tensors):
            mine[t, tile] = product[t * tile_rows:(t + 1) * tile_rows]
        for k in range(1, tensors):
            y_copy(k, tile).start()
        return carry

    lax.fori_loop(0, tiles, project, 0)

    def add_up(tile, carry):
        cols = pl.ds(pl.multiple_of(tile * tile_cols, tile_cols), tile_cols)
        total = mine[rank_t, tile].astype(jnp.float32)
        for k in range(1, tensors):
            y_copy(tensors - k, tile).wait_recv()
            total += theirs[k, tile].astype(jnp.float32)
        out_ref[:, cols] = total.astype(jnp.bfloat16)
        for k in range(1, tensors):
            y_copy(k, tile).wait_send()
        return carry

    lax.fori_loop(0, tiles, add_up, 0)

    def sent(i, carry):
        for way in range(2):
            passed = i >= plane if way == 0 else i <= plane

            @pl.when(passed & has_next(way))
            def _(way=way):
                q_copy(way, i).wait_send()

        @pl.when(i != plane)
        def _():
            for k in range(heads_kv):
                part_copy(0, i, k).wait_send()
                stat_copy(0, i, k).wait_send()
        return carry

    lax.fori_loop(0, planes, sent, 0)
    for j in range(1, members - 1 if square else members):
        kv_copy(j).wait_send()
    if square:
        for half in range(2):
            corner_copy(half).wait_send()


def local(queries, new_kv, cache, block_owner, block_slot, prefix_blocks, out_weight):
    replicas = lax.axis_size("replica")
    own = lax.axis_index("replica")
    capacity = max(2, MAXB // replicas)
    planes = math.isqrt(replicas)
    members = replicas // planes
    tokens, heads_kv = queries.shape[0], cache.shape[3] // HD
    lanes = PER_GROUP * tokens
    slots, counts = block_tables(
        block_owner, block_slot, prefix_blocks, own, planes, members, capacity)
    part = (planes, heads_kv, HD, lanes)
    stats = (planes, heads_kv, 2, lanes)
    vmem = pl.BlockSpec(memory_space=pltpu.VMEM)
    smem = pl.BlockSpec(memory_space=pltpu.SMEM)
    pairs = replicas * capacity * BLOCK * heads_kv * lanes
    tensors, width = lax.axis_size("tensor"), out_weight.shape[1]
    tile_cols = min(512, width)
    halves = (tensors, width // tile_cols, tokens // tensors, tile_cols)
    anywhere = pl.BlockSpec(memory_space=pl.ANY)
    return pl.pallas_call(
        functools.partial(attend_kernel, planes, members, capacity),
        out_shape=jax.ShapeDtypeStruct((tokens // tensors, width), jnp.bfloat16),
        in_specs=[smem, smem, anywhere, anywhere, anywhere, anywhere],
        out_specs=vmem,
        scratch_shapes=[
            *[pltpu.VMEM(a.shape, jnp.bfloat16) for a in (queries, new_kv, cache, out_weight)],
            pltpu.VMEM(queries.shape, jnp.bfloat16),
            pltpu.VMEM(halves, jnp.bfloat16),
            pltpu.VMEM(halves, jnp.bfloat16),
            pltpu.SemaphoreType.DMA((4,)),
            pltpu.SemaphoreType.DMA(halves[:2]),
            pltpu.SemaphoreType.DMA(halves[:2]),
            pltpu.VMEM((planes, heads_kv, lanes, HD), jnp.bfloat16),
            [pltpu.VMEM(cache.shape, jnp.bfloat16) for _ in range(members - 1)],
            pltpu.VMEM(part, jnp.float32),
            pltpu.VMEM(stats, jnp.float32),
            pltpu.VMEM(part, jnp.bfloat16),
            pltpu.VMEM((2, *part), jnp.bfloat16),
            pltpu.VMEM((2, *stats), jnp.float32),
            pltpu.SemaphoreType.DMA((2, planes)),
            pltpu.SemaphoreType.DMA((planes,)),
            pltpu.SemaphoreType.DMA((members + 1,)),
            pltpu.SemaphoreType.DMA((members + 1,)),
            pltpu.SemaphoreType.DMA((planes, heads_kv)),
            pltpu.SemaphoreType.DMA((2, planes, heads_kv)),
            pltpu.SemaphoreType.DMA((planes, heads_kv)),
            pltpu.SemaphoreType.DMA((2, planes, heads_kv)),
        ],
        compiler_params=pltpu.CompilerParams(
            collective_id=0, has_side_effects=True, vmem_limit_bytes=56 * 1024 * 1024),
        cost_estimate=pl.CostEstimate(
            flops=4 * pairs * HD, bytes_accessed=4 * cache.size + 2 * out_weight.size, transcendentals=pairs),
    )(slots, counts, queries, new_kv, cache, out_weight)


def solution(mesh):
    placed = (
        P("replica", "tensor"),
        P(None, "replica", "tensor"),
        P("replica", None, None, "tensor"),
        P(),
        P(),
        P(),
        P("tensor", None),
    )
    return jax.shard_map(
        local, mesh=mesh, in_specs=placed, out_specs=P(("replica", "tensor"), None), check_vma=False
    )
```
